256 devices in a mesh: dp: 32 (over z, y_hi, core), expert: 8 (over y_lo, x).
Axes of the slice: x: 4, y: 4 (y_hi: 2, y_lo: 2; y = y_hi * 2 + y_lo), z: 8, core: 2. Of those that a mesh axis runs over, the one named last changes fastest.
Arguments:
- tokens: bfloat16 [1024, 7168], P('dp', 'expert'), may hold values from -6 to 6
- cotangent: bfloat16 [1024, 7168], P('dp', 'expert'), may hold values from -0.75 to 0.75
- route_ids: int32 [1024, 2], replicated, may hold values from 0 to 3, all different within a row; in each aligned block of 1024 rows (0 to 1023, 1024 to 2047, ...) at most 640 rows name the same one
- route_probs: float32 [1024, 2], replicated, may hold values from 0.25 to 1
- dense_gate: bfloat16 [7168, 4864], P('expert', 'dp'), may hold values from -0.0625 to 0.0625
- dense_up: bfloat16 [7168, 4864], P('expert', 'dp'), may hold values from -0.0625 to 0.0625
- dense_down: bfloat16 [4864, 7168], P('dp', 'expert'), may hold values from -0.078125 to 0.078125
- expert_gate: bfloat16 [7168, 19456], P('expert', 'dp'), may hold values from -0.0625 to 0.0625
- expert_up: bfloat16 [7168, 19456], P('expert', 'dp'), may hold values from -0.0625 to 0.0625
- expert_down: bfloat16 [19456, 7168], P('dp', 'expert'), may hold values from -0.078125 to 0.078125
Outputs:
- input_grad: float32 [1024, 7168], P('dp', 'expert')
- dense_gate_grad: float32 [7168, 4864], P('expert', 'dp')
- dense_up_grad: float32 [7168, 4864], P('expert', 'dp')
- dense_down_grad: float32 [4864, 7168], P('dp', 'expert')
- expert_gate_grad: float32 [7168, 19456], P('expert', 'dp')
- expert_up_grad: float32 [7168, 19456], P('expert', 'dp')
- expert_down_grad: float32 [19456, 7168], P('dp', 'expert')
The draws below stay inside these ranges and needn't reach their ends.
Inputs may be any that keep to these rules, and one draw needn't show every extreme that they name: `route_ids`: each row names two different experts; no expert is named by more than 640 rows, a bound that some block reaches.
All inputs are finite; a program needn't handle non-finite values.
Results may differ from the reference program's by a relative error of at most 0.0029.
Values may be sent and summed in bfloat16 or wider, within the bound.
No kernel may reach another device: no remote copies, remote signals or barrier semaphores. Data moves between devices by JAX's collectives and lax.ppermute only.
A program may use at most 128 MiB of HBM per device.

```python
import math
import jax
import jax.numpy as jnp
import numpy as np

D = 7168
FF = 4864
EXPERTS = 4
TOKENS = 1024
CAP = 640


def block_scale(stream_key, dims, shards, least, largest):
    def one(axis_at, blocks):
        steps = jax.random.uniform(jax.random.fold_in(jax.random.fold_in(stream_key, 6), axis_at), (blocks,), jnp.float32, least / len(shards), largest / len(shards))
        return jnp.repeat(jnp.exp(steps), dims[axis_at] // blocks).reshape((-1,) + (1,) * (len(dims) - axis_at - 1))

    gain = one(*shards[0])
    for cut in shards[1:]:
        gain = gain * one(*cut)
    return gain


def routed_block(stream_key, own, number, rows, number_of, top, most, skew):
    sequence = jax.random.permutation(stream_key, number_of)
    packed, common = load_shares(number_of, rows * top, most, skew, True), load_shares(number_of, rows * top, most, skew, False)
    places = jnp.arange(number_of)

    def named(lengths, rotation):
        used = int((lengths > 0).sum())
        fixed = max(1, used // 4)
        shifted = fixed + (places - fixed + rotation * (used - fixed)) % max(1, number_of - fixed)
        return jnp.zeros((number_of,), jnp.int32).at[sequence[jnp.where(places < fixed, places, shifted)]].set(jnp.asarray(lengths, jnp.int32))

    lengths = jnp.where(number % 4 == 0, named(packed, number // 4), named(common, number - number // 4 - 1))
    mixed = jax.random.permutation(jax.random.fold_in(own, 3), number_of)
    source_of, receiver = mixed[0:number_of // 2 * 2:2], mixed[1:number_of // 2 * 2:2]
    slack = jnp.minimum(lengths[source_of] - 1, most - lengths[receiver]) // 2
    slack = jnp.where((source_of == sequence[0]) | (receiver == sequence[0]) | (lengths[receiver] == 0), 0, jnp.maximum(slack, 0))
    shifted = jax.random.randint(jax.random.fold_in(own, 4), (number_of // 2,), 0, 1 << 20) % (slack + 1)
    lengths = lengths.at[source_of].add(-shifted).at[receiver].add(shifted)
    items = jnp.searchsorted(jnp.cumsum(lengths), jnp.arange(rows * top), side="right").astype(jnp.int32)
    table = items.reshape(top, rows).T
    table = table[jax.random.permutation(jax.random.fold_in(own, 1), rows)]
    rotation = jax.random.randint(jax.random.fold_in(own, 2), (rows, 1), 0, top)
    return jnp.take_along_axis(table, (jnp.arange(top)[None, :] + rotation) % top, axis=1)


def load_shares(count, total, reach, slope, full):
    loads = [(1 << 20) // math.isqrt(standing ** slope) + 1 for standing in range(1, count + 1)]
    largest = reach if full else min(reach, max(-(-total // count), total * loads[0] // sum(loads)))
    least = 1 if total - largest >= count - 1 else 0
    holding, surplus = [largest] + [least] * (count - 1), total - largest - least * (count - 1)
    while surplus > 0:
        free = [i for i in range(1, count) if holding[i] < largest] or [i for i in range(1, count) if holding[i] < reach]
        mass, remaining = sum([loads[i] for i in free]), surplus
        for i in free:
            more = min(reach - holding[i], max(1, remaining * loads[i] // mass), surplus)
            holding[i] = holding[i] + more
            surplus = surplus - more
    return np.array(holding)


def centred(key, extent, width, reach, cuts=(), kind=jnp.bfloat16):
    factor_of = block_scale(key, extent, cuts, -0.22, 0.18) if cuts else 1.0
    entries = jax.random.normal(key, extent, jnp.float32) * width * factor_of
    return jnp.minimum(jnp.maximum(entries, -reach), reach).astype(kind)


def setup_inputs(seed: int = 0) -> dict:
    keys = jax.random.split(jax.random.key(seed), 11)
    tokens = centred(keys[0], (TOKENS, D), 1.0, 6.0, ((0, 32), (1, 8)))
    cotangent = centred(keys[1], (TOKENS, D), 0.125, 0.75, ((0, 32), (1, 8)))
    route_ids_keys = jax.random.split(jax.random.fold_in(keys[2], 1), TOKENS // TOKENS)
    route_ids_turns = jax.random.permutation(jax.random.fold_in(keys[2], 3), TOKENS // TOKENS)
    route_ids = jax.vmap(lambda own, number: routed_block(jax.random.fold_in(keys[2], 2), own, number, TOKENS, EXPERTS, 2, CAP, 1))(route_ids_keys, route_ids_turns).reshape((TOKENS, 2))
    route_probs = jnp.clip(jax.random.uniform(keys[3], (TOKENS, 2), jnp.float32, 0.25, 1.0), 0.25, 1.0)
    dense_gate = centred(keys[4], (D, FF), D ** -0.5, 0.0625, ((0, 8), (1, 32)))
    dense_up = centred(keys[5], (D, FF), D ** -0.5, 0.0625, ((0, 8), (1, 32)))
    dense_down = centred(keys[6], (FF, D), FF ** -0.5, 0.078125, ((0, 32), (1, 8)))
    expert_gate = centred(keys[7], (D, EXPERTS * FF), D ** -0.5, 0.0625, ((0, 8), (1, 32)))
    expert_up = centred(keys[8], (D, EXPERTS * FF), D ** -0.5, 0.0625, ((0, 8), (1, 32)))
    expert_down = centred(keys[9], (EXPERTS * FF, D), FF ** -0.5, 0.078125, ((0, 32), (1, 8)))
    return dict(tokens=tokens, cotangent=cotangent, route_ids=route_ids, route_probs=route_probs, dense_gate=dense_gate, dense_up=dense_up, dense_down=dense_down, expert_gate=expert_gate, expert_up=expert_up, expert_down=expert_down)


def slot_table(route_ids, route_probs, expert_number, capacity):
    chosen = route_ids == expert_number
    member = jnp.any(chosen, axis=1)
    token_weight = jnp.sum(jnp.where(chosen, route_probs, jnp.zeros_like(route_probs)), axis=1)
    position = jnp.cumsum(member.astype(jnp.int32)) - 1
    target = jnp.where(member, position, capacity).astype(jnp.int32)
    order = jnp.arange(route_ids.shape[0], dtype=jnp.int32)
    slot_token = jnp.zeros((capacity,), jnp.int32).at[target].set(order, mode="drop")
    slot_weight = jnp.zeros((capacity,), route_probs.dtype).at[target].set(token_weight, mode="drop")
    return slot_token, slot_weight


def swiglu_terms(gate_part, up_part, back_part, weight):
    sigmoid_gate = jax.nn.sigmoid(gate_part)
    lifted = gate_part * sigmoid_gate
    weighted = (weight * lifted * up_part).astype(jnp.bfloat16)
    grad_act = weight * back_part
    grad_gate = (grad_act * up_part * sigmoid_gate * (1.0 + gate_part * (1.0 - sigmoid_gate))).astype(jnp.bfloat16)
    grad_up = (grad_act * lifted).astype(jnp.bfloat16)
    return weighted, grad_gate, grad_up


def reference(tokens, cotangent, route_ids, route_probs, dense_gate, dense_up, dense_down, expert_gate, expert_up, expert_down):
    gate_part = jnp.dot(tokens, dense_gate, preferred_element_type=jnp.float32)
    up_part = jnp.dot(tokens, dense_up, preferred_element_type=jnp.float32)
    back_part = jnp.dot(cotangent, dense_down.T, preferred_element_type=jnp.float32)
    weighted, grad_gate, grad_up = swiglu_terms(gate_part, up_part, back_part, 1.0)
    dense_gate_grad = jnp.dot(tokens.T, grad_gate, preferred_element_type=jnp.float32)
    dense_up_grad = jnp.dot(tokens.T, grad_up, preferred_element_type=jnp.float32)
    dense_down_grad = jnp.dot(weighted.T, cotangent, preferred_element_type=jnp.float32)
    input_grad = jnp.dot(grad_gate, dense_gate.T, preferred_element_type=jnp.float32)
    input_grad = input_grad + jnp.dot(grad_up, dense_up.T, preferred_element_type=jnp.float32)
    gate_blocks = []
    up_blocks = []
    down_blocks = []
    for expert_number in range(EXPERTS):
        first = expert_number * FF
        w_gate = expert_gate[:, first:first + FF]
        w_up = expert_up[:, first:first + FF]
        w_down = expert_down[first:first + FF, :]
        slot_token, slot_weight = slot_table(route_ids, route_probs, expert_number, CAP)
        rows_in = tokens[slot_token]
        rows_back = cotangent[slot_token]
        gate_rows = jnp.dot(rows_in, w_gate, preferred_element_type=jnp.float32)
        up_rows = jnp.dot(rows_in, w_up, preferred_element_type=jnp.float32)
        back_rows = jnp.dot(rows_back, w_down.T, preferred_element_type=jnp.float32)
        weighted_e, grad_gate_e, grad_up_e = swiglu_terms(gate_rows, up_rows, back_rows, slot_weight[:, None])
        gate_blocks.append(jnp.dot(rows_in.T, grad_gate_e, preferred_element_type=jnp.float32))
        up_blocks.append(jnp.dot(rows_in.T, grad_up_e, preferred_element_type=jnp.float32))
        down_blocks.append(jnp.dot(weighted_e.T, rows_back, preferred_element_type=jnp.float32))
        expert_in = jnp.dot(grad_gate_e, w_gate.T, preferred_element_type=jnp.float32)
        expert_in = expert_in + jnp.dot(grad_up_e, w_up.T, preferred_element_type=jnp.float32)
        input_grad = input_grad.at[slot_token].add(expert_in)
    expert_gate_grad = jnp.concatenate(gate_blocks, axis=1)
    expert_up_grad = jnp.concatenate(up_blocks, axis=1)
    expert_down_grad = jnp.concatenate(down_blocks, axis=0)
    return (input_grad, dense_gate_grad, dense_up_grad, dense_down_grad, expert_gate_grad, expert_up_grad, expert_down_grad)
```

```python
import jax
import jax.numpy as jnp
from jax import lax
from jax.experimental import pallas as pl
from jax.experimental.pallas import tpu as pltpu
from jax.sharding import Mesh, PartitionSpec as P

FF = 4864
Z, YH, C, YL, X = 8, 2, 2, 2, 4
AXES = ("z", "yh", "c", "yl", "x")
SIZES = (Z, YH, C, YL, X)
DP = ("z", "yh", "c")
EX = ("yl", "x")
PARTS = YL * X
F32 = jnp.float32
BF16 = jnp.bfloat16
TOKENS, CAP, WIDTH = 1024, 640, 896
HE, HD = 608, 152
QUARTER = 256
STRIDE = 160
SHARE = 80
BLOCK = 3 * SHARE
CODED = BLOCK + 16
OWN = 32
VMEM = 40 * 1024 * 1024


def dot(left, right, dims):
    return lax.dot_general(left, right, ((dims[:1], dims[1:]), ((), ())), preferred_element_type=F32)


def shape(dims, kind):
    return jax.ShapeDtypeStruct(dims, kind)


def shift(value, axis, size, step):
    return lax.ppermute(value, axis, [(i, (i + step) % size) for i in range(size)])


def gather_column(own):
    pair = jnp.stack([own, shift(own, "yh", YH, 1)])
    pieces = [pair]
    below, above = pair, pair
    for _ in range(Z // 2 - 1):
        below, above = shift(below, "z", Z, 1), shift(above, "z", Z, -1)
        pieces += [below, above]
    pieces += [shift(below[:1], "z", Z, 1), shift(above[1:], "z", Z, -1)]
    return jnp.concatenate(pieces)


def gather_terms(value, first):
    if first == "x":
        near = [value, shift(value, "x", X, 1), shift(value, "x", X, -1), shift(value, "x", X, 2)]
        return [v[None] for v in near + [shift(v, "yl", YL, 1) for v in near]]
    pair = jnp.stack([value, shift(value, "yl", YL, 1)])
    return [pair, shift(pair, "x", X, 1), shift(pair, "x", X, -1), shift(pair, "x", X, 2)]


FROM_X = (0, -1, 1, 2)
RELATIVE = {
    "x": [[(r, k)] for r in range(YL) for k in FROM_X],
    "yl": [[(0, k), (1, k)] for k in FROM_X],
}
FROM_Z = (0, -1, 1, -2, 2, -3, 3, 4)


def place_terms(place_ref, blocks, first, to_ref):
    yl, x = place_ref[3], place_ref[4]
    for block, origins in zip(blocks, RELATIVE[first]):
        for i, (row, away) in enumerate(origins):
            j = lax.rem(yl + row, YL) * X + lax.rem(x + away + X, X)
            to_ref[pl.ds(pl.multiple_of(j * SHARE, SHARE), SHARE), :] = block[i]


def forward_kernel(place_ref, pos_ref, mine_ref, sibling_ref, *refs):
    far_weights, far_rows, out_ref = refs[:6], refs[6:10], refs[10]
    weights, rows, sums_ref, in_sems, out_sems = refs[11:17], refs[17:21], refs[21], refs[22], refs[23]
    tok_ref, cot_ref, in_ref, back_ref = rows
    weights_e, weights_d = weights[0:6:2], weights[1:6:2]
    fetches = [pltpu.make_async_copy(far, near, in_sems.at[i]) for i, (far, near) in enumerate(zip(far_weights, weights))]
    stores = [pltpu.make_async_copy(near, far, out_sems.at[i]) for i, (near, far) in enumerate(zip(rows, far_rows))]
    for fetch in fetches:
        fetch.start()
    z, yh, c = place_ref[0], place_ref[1], place_ref[2]
    for core, column in enumerate((mine_ref, sibling_ref)):
        for k, away in enumerate(FROM_Z):
            for r in range(YH):
                at = lax.rem(z + away + Z, Z) * (YH * C * OWN) + lax.rem(yh + r, YH) * (C * OWN) + lax.rem(c + core, C) * OWN
                at = pl.multiple_of(at, OWN)
                tok_ref[pl.ds(at, OWN), :] = column[YH * k + r, 0]
                cot_ref[pl.ds(at, OWN), :] = column[YH * k + r, 1]
    slots = lax.broadcasted_iota(jnp.int32, (CAP, TOKENS), 0)
    one_hot = jnp.where(slots == pos_ref[...], 1.0, 0.0).astype(BF16)
    in_ref[...] = dot(one_hot, tok_ref[...], (1, 0)).astype(BF16)
    back_ref[...] = dot(one_hot, cot_ref[...], (1, 0)).astype(BF16)
    for store in stores:
        store.start()
    exponents = [[] for _ in range(PARTS)]
    for k in range(3):
        picked, whole = (back_ref, cot_ref) if k == 2 else (in_ref, tok_ref)
        fetches[2 * k].wait()
        fetches[2 * k + 1].wait()
        sums_ref[0:HE, 0:CAP] = dot(weights_e[k][...], picked[...], (1, 1))
        sums_ref[HE:, 0:CAP] = jnp.zeros((PARTS * SHARE - HE, CAP), F32)
        dense = dot(weights_d[k][...], whole[...], (1, 1))
        for q in range(TOKENS // QUARTER):
            sums_ref[q * STRIDE : q * STRIDE + HD, CAP:] = dense[:, q * QUARTER : (q + 1) * QUARTER]
            sums_ref[q * STRIDE + HD : (q + 1) * STRIDE, CAP:] = jnp.zeros((STRIDE - HD, QUARTER), F32)
        for j in range(PARTS):
            block = sums_ref[j * SHARE : (j + 1) * SHARE, :]
            largest = jnp.maximum(jnp.max(jnp.abs(block), axis=0, keepdims=True), 1e-30)
            exponent = jnp.ceil(jnp.log2(largest) + 1e-3)
            coded = jnp.round(block * jnp.exp2(15.0 - exponent))
            coded = jnp.minimum(jnp.maximum(coded, -32767.0), 32767.0)
            out_ref[j, k * SHARE : (k + 1) * SHARE, :] = coded.astype(jnp.int32).astype(jnp.int16)
            exponents[j].append(exponent)
    row = lax.broadcasted_iota(jnp.int32, (CODED - BLOCK, WIDTH), 0)
    for j in range(PARTS):
        tile = jnp.where(row == 0, exponents[j][0], jnp.where(row == 1, exponents[j][1], exponents[j][2]))
        out_ref[j, BLOCK:, :] = tile.astype(jnp.int32).astype(jnp.int16)
    for store in stores:
        store.wait()


def terms_kernel(in_ref, weight_ref, weighted_ref, gate_ref, up_ref):
    totals = []
    for k in range(3):
        total = jnp.zeros((SHARE, WIDTH), F32)
        for j in range(PARTS):
            exponent = in_ref[j, BLOCK:, :].astype(jnp.int32).astype(F32)[k : k + 1]
            total = total + in_ref[j, k * SHARE : (k + 1) * SHARE, :].astype(jnp.int32).astype(F32) * jnp.exp2(exponent - 15.0)
        totals.append(total)
    gate, up, back = totals
    weight = weight_ref[...]
    sigmoid_gate = 1.0 / (1.0 + jnp.exp(-gate))
    lifted = gate * sigmoid_gate
    grad_act = weight * back
    weighted_ref[...] = (weight * lifted * up).astype(BF16)
    gate_ref[...] = (grad_act * up * sigmoid_gate * (1.0 + gate * (1.0 - sigmoid_gate))).astype(BF16)
    up_ref[...] = (grad_act * lifted).astype(BF16)


def input_kernel(place_ref, pos_ref, *refs):
    blocks, refs = refs[:12], refs[12:]
    gate_e, gate_d, up_e, up_d, kept_ref, sent_ref, gate_ref, up_ref, total_ref = refs
    c = place_ref[2]
    place_terms(place_ref, blocks[:8], "x", gate_ref)
    place_terms(place_ref, blocks[8:], "yl", up_ref)
    gate, up = gate_ref[...], up_ref[...]
    routed = dot(gate[0:HE, 0:CAP], gate_e[...], (0, 0)) + dot(up[0:HE, 0:CAP], up_e[...], (0, 0))
    high = routed.astype(BF16)
    low = (routed - high.astype(F32)).astype(BF16)
    slots = lax.broadcasted_iota(jnp.int32, (TOKENS, CAP), 1)
    one_hot = jnp.where(slots == pos_ref[...], 1.0, 0.0).astype(BF16)
    total_ref[...] = dot(one_hot, high, (1, 0)) + dot(one_hot, low, (1, 0))
    for q in range(TOKENS // QUARTER):
        rows = slice(q * STRIDE, q * STRIDE + HD)
        dense = dot(gate[rows, CAP:], gate_d[...], (0, 0)) + dot(up[rows, CAP:], up_d[...], (0, 0))
        total_ref[q * QUARTER : (q + 1) * QUARTER, :] += dense
    for i in range(Z * YH):
        mine = pl.multiple_of(i * C * OWN + c * OWN, OWN)
        other = pl.multiple_of(i * C * OWN + (1 - c) * OWN, OWN)
        kept_ref[i] = total_ref[pl.ds(mine, OWN), :]
        sent_ref[i] = total_ref[pl.ds(other, OWN), :].astype(BF16)


def weights_kernel(place_ref, gate_ref, up_ref, *refs):
    blocks, (tok_ref, cot_ref, in_ref, back_ref), outs, down_ref = refs[:4], refs[4:8], refs[8:14], refs[14]
    place_terms(place_ref, blocks, "yl", down_ref)
    for k, (value_ref, rows, whole) in enumerate(((gate_ref, in_ref, tok_ref), (up_ref, in_ref, tok_ref), (down_ref, back_ref, cot_ref))):
        dense = jnp.concatenate([value_ref[q * STRIDE : q * STRIDE + HD, CAP:] for q in range(TOKENS // QUARTER)], axis=1)
        outs[k][...] = dot(dense, whole[...], (1, 0))
        outs[k + 3][...] = dot(value_ref[0:HE, 0:CAP], rows[...], (1, 0))


def shards(tokens, cotangent, route_ids, route_probs, dense_gate, dense_up, dense_down, expert_gate, expert_up, expert_down):
    expert_number = lax.axis_index(DP) * HE // FF
    place = jnp.stack([lax.axis_index(a) for a in AXES]).astype(jnp.int32)
    smem = pl.BlockSpec(memory_space=pltpu.SMEM)

    chosen = route_ids == expert_number
    member = jnp.any(chosen, axis=1)
    token_weight = jnp.sum(jnp.where(chosen, route_probs, 0.0), axis=1)
    position = jnp.where(member, jnp.cumsum(member.astype(jnp.int32)) - 1, -1)
    slots = lax.broadcasted_iota(jnp.int32, (CAP, TOKENS), 0)
    slot_weight = jnp.sum(jnp.where(slots == position[None, :], token_weight[None, :], 0.0), axis=1)
    weight = jnp.concatenate([slot_weight, jnp.ones((QUARTER,), F32)])[None, :]

    mine_column = gather_column(jnp.stack([tokens, cotangent]))
    across, down = lax.optimization_barrier((position[None, :], position[:, None]))
    sibling_column = shift(mine_column, "c", C, 1)
    gate_e, gate_d, up_e, up_d = expert_gate.T, dense_gate.T, expert_up.T, dense_up.T

    far, vmem = pl.BlockSpec(memory_space=pl.ANY), pl.BlockSpec(memory_space=pltpu.VMEM)
    params = pltpu.CompilerParams(vmem_limit_bytes=VMEM)
    small, large = (HD, WIDTH), (HE, WIDTH)
    whole, picked, share = (TOKENS, WIDTH), (CAP, WIDTH), (SHARE, WIDTH)
    held = [(large, BF16), (small, BF16)] * 3 + [(whole, BF16)] * 2 + [(picked, BF16)] * 2
    all_tokens, all_grads, rows_in, rows_back, coded = pl.pallas_call(
        forward_kernel,
        out_shape=[shape(*h) for h in held[6:]] + [shape((PARTS, CODED, WIDTH), jnp.int16)],
        in_specs=[smem, vmem, vmem, vmem] + [far] * 6,
        out_specs=[far] * 4 + [vmem],
        scratch_shapes=[pltpu.VMEM(*h) for h in held]
        + [pltpu.VMEM((PARTS * SHARE, WIDTH), F32), pltpu.SemaphoreType.DMA((6,)), pltpu.SemaphoreType.DMA((4,))],
        compiler_params=params,
        name="forward",
    )(place, across, mine_column, sibling_column, gate_e, gate_d, up_e, up_d, expert_down, dense_down)
    arrived = lax.all_to_all(coded, EX, 0, 0)
    weighted, grad_gate, grad_up = pl.pallas_call(
        terms_kernel,
        out_shape=[shape(share, BF16)] * 3,
        compiler_params=params,
        name="terms",
    )(arrived, weight)

    part = (Z * YH, OWN, WIDTH)
    summed = (PARTS * SHARE, WIDTH)
    kept, sent, gate_terms, up_terms = pl.pallas_call(
        input_kernel,
        out_shape=[shape(part, F32), shape(part, BF16), shape(summed, BF16), shape(summed, BF16)],
        in_specs=[smem] + [vmem] * 17,
        scratch_shapes=[pltpu.VMEM(whole, F32)],
        compiler_params=params,
        name="input",
    )(place, down, *gather_terms(grad_gate, "x"), *gather_terms(grad_up, "yl"), gate_e, gate_d, up_e, up_d)
    sent, weighted = lax.optimization_barrier((sent, weighted))
    chip = (kept + shift(sent, "c", C, 1).astype(F32)).astype(BF16)
    weighted_terms = gather_terms(weighted, "yl")
    input_grad = jnp.sum(lax.all_to_all(chip, ("z", "yh"), 0, 0).astype(F32), axis=0)

    grads = pl.pallas_call(
        weights_kernel,
        out_shape=[shape(small, F32)] * 3 + [shape(large, F32)] * 3,
        in_specs=[smem] + [vmem] * 10,
        scratch_shapes=[pltpu.VMEM(summed, BF16)],
        compiler_params=params,
        name="weights",
    )(place, gate_terms, up_terms, *weighted_terms, all_tokens, all_grads, rows_in, rows_back)
    return (input_grad, grads[0].T, grads[1].T, grads[2], grads[3].T, grads[4].T, grads[5])


def solution(mesh):
    fine = Mesh(mesh.devices.reshape(SIZES), AXES)
    rows, cols = P(DP, EX), P(EX, DP)
    in_specs = (rows, rows, P(), P(), cols, cols, rows, cols, cols, rows)
    out_specs = (rows, cols, cols, rows, cols, cols, rows)
    return jax.shard_map(shards, mesh=fine, in_specs=in_specs, out_specs=out_specs, check_vma=False)
```

```python
import jax
import jax.numpy as jnp
from jax import lax
from jax.experimental import pallas as pl
from jax.experimental.pallas import tpu as pltpu
from jax.sharding import Mesh, PartitionSpec as P

FF = 4864
Z, YH, C, YL, X = 8, 2, 2, 2, 4
AXES = ("z", "yh", "c", "yl", "x")
SIZES = (Z, YH, C, YL, X)
DP = ("z", "yh", "c")
EX = ("yl", "x")
PARTS = YL * X
F32 = jnp.float32
BF16 = jnp.bfloat16
TOKENS, CAP, WIDTH = 1024, 640, 896
HE, HD = 608, 152
QUARTER = 256
STRIDE = 160
SHARE = 80
BLOCK = 3 * SHARE
CODED = BLOCK + 16
OWN = 32
SPLIT = 384
MIB = 1024 * 1024


def dot(left, right, dims):
    return lax.dot_general(left, right, ((dims[:1], dims[1:]), ((), ())), preferred_element_type=F32)


def shape(dims, kind):
    return jax.ShapeDtypeStruct(dims, kind)


def shift(value, axis, size, step):
    return lax.ppermute(value, axis, [(i, (i + step) % size) for i in range(size)])


def gather_column(own, *others):
    pair = jnp.stack([own, shift(own, "yh", YH, 1)])
    pieces = [pair]
    below, above = pair, pair
    for step in range(Z // 2 - 1):
        below, above = shift(below, "z", Z, 1), shift(above, "z", Z, -1)
        if step == 1:
            below, above, *others = lax.optimization_barrier((below, above, *others))
        pieces += [below, above]
    last = [shift(below[:1], "z", Z, 1), shift(above[1:], "z", Z, -1)]
    return jnp.concatenate(pieces), jnp.concatenate(last), *others


def gather_terms(value, first):
    if first == "x":
        near = [value, shift(value, "x", X, 1), shift(value, "x", X, -1), shift(value, "x", X, 2)]
        return [v[None] for v in near + [shift(v, "yl", YL, 1) for v in near]]
    return gather_pairs(jnp.stack([value, shift(value, "yl", YL, 1)]))


def gather_pairs(pair):
    return [pair, shift(pair, "x", X, 1), shift(pair, "x", X, -1), shift(pair, "x", X, 2)]


FROM_X = (0, -1, 1, 2)
TO_X = (0, 1, -1, 2)
TO_Z = (4, 3, 5, 2, 6, 1, 7)
RELATIVE = {
    "x": [[(r, k)] for r in range(YL) for k in FROM_X],
    "yl": [[(0, k), (1, k)] for k in FROM_X],
}
FROM_Z = (0, -1, 1, -2, 2, -3, 3, 4)


def place_terms(place_ref, blocks, first, to_ref):
    yl, x = place_ref[3], place_ref[4]
    for block, origins in zip(blocks, RELATIVE[first]):
        for i, (row, away) in enumerate(origins):
            j = lax.rem(yl + row, YL) * X + lax.rem(x + away + X, X)
            to_ref[pl.ds(pl.multiple_of(j * SHARE, SHARE), SHARE), :] = block[i]


def encode(value, to, k):
    largest = jnp.maximum(jnp.max(jnp.abs(value), axis=0, keepdims=True), 1e-30)
    exponent = jnp.ceil(jnp.log2(largest) + 1e-3)
    coded = jnp.round(value * jnp.exp2(15.0 - exponent))
    to[k * SHARE : (k + 1) * SHARE, :] = coded.astype(jnp.int32).astype(jnp.int16)
    return exponent


def encode_exponents(exponents, to):
    row = lax.broadcasted_iota(jnp.int32, (CODED - BLOCK, exponents[0].shape[1]), 0)
    tile = jnp.where(row == 0, exponents[0], jnp.where(row == 1, exponents[1], exponents[2]))
    to[BLOCK:, :] = tile.astype(jnp.int32).astype(jnp.int16)


def decode(coded, k):
    exponent = coded[BLOCK:, :].astype(jnp.int32).astype(F32)[k : k + 1]
    return coded[k * SHARE : (k + 1) * SHARE, :].astype(jnp.int32).astype(F32) * jnp.exp2(exponent - 15.0)


def forward_kernel(place_ref, pos_ref, mine_ref, mine_far_ref, sibling_ref, sibling_far_ref, *refs):
    far_weights, far_rows = refs[:6], refs[6:10]
    kept_a, sent_a, sent_b = refs[10], refs[11], refs[12:16]
    weights, rows, sums_ref, in_sems, out_sems = refs[16:22], refs[22:26], refs[26], refs[27], refs[28]
    tok_ref, cot_ref, in_ref, back_ref = rows
    weights_e, weights_d = weights[0:6:2], weights[1:6:2]
    fetches = [pltpu.make_async_copy(far, near, in_sems.at[i]) for i, (far, near) in enumerate(zip(far_weights, weights))]
    stores = [pltpu.make_async_copy(near, far, out_sems.at[i]) for i, (near, far) in enumerate(zip(rows, far_rows))]
    for fetch in fetches:
        fetch.start()
    z, yh, c = place_ref[0], place_ref[1], place_ref[2]
    yl, x = place_ref[3], place_ref[4]
    for core, columns in enumerate(((mine_ref, mine_far_ref), (sibling_ref, sibling_far_ref))):
        for k, away in enumerate(FROM_Z):
            for r in range(YH):
                at = lax.rem(z + away + Z, Z) * (YH * C * OWN) + lax.rem(yh + r, YH) * (C * OWN) + lax.rem(c + core, C) * OWN
                at = pl.multiple_of(at, OWN)
                column, i = (columns[0], YH * k + r) if k < Z - 1 else (columns[1], r)
                tok_ref[pl.ds(at, OWN), :] = column[i, 0]
                cot_ref[pl.ds(at, OWN), :] = column[i, 1]
    slots = lax.broadcasted_iota(jnp.int32, (CAP, TOKENS), 0)
    one_hot = jnp.where(slots == pos_ref[...], 1.0, 0.0).astype(BF16)
    in_ref[...] = dot(one_hot, tok_ref[...], (1, 0)).astype(BF16)
    back_ref[...] = dot(one_hot, cot_ref[...], (1, 0)).astype(BF16)
    for store in stores:
        store.start()
    targets = []
    for r in range(YL):
        for i, away in enumerate(TO_X):
            j = lax.rem(yl + r, YL) * X + lax.rem(x + away + X, X)
            to_a, to_b = (sent_a if r else kept_a).at[i], sent_b[i].at[r]
            targets.append((pl.multiple_of(j * SHARE, SHARE), to_a, to_b, [], []))
    for k in range(3):
        picked, whole = (back_ref, cot_ref) if k == 2 else (in_ref, tok_ref)
        fetches[2 * k].wait()
        fetches[2 * k + 1].wait()
        sums_ref[0:HE, 0:CAP] = dot(weights_e[k][...], picked[...], (1, 1))
        sums_ref[HE:, 0:CAP] = jnp.zeros((PARTS * SHARE - HE, CAP), F32)
        dense = dot(weights_d[k][...], whole[...], (1, 1))
        for q in range(TOKENS // QUARTER):
            sums_ref[q * STRIDE : q * STRIDE + HD, CAP:] = dense[:, q * QUARTER : (q + 1) * QUARTER]
            sums_ref[q * STRIDE + HD : (q + 1) * STRIDE, CAP:] = jnp.zeros((STRIDE - HD, QUARTER), F32)
        for at, to_a, to_b, exponents_a, exponents_b in targets:
            block = sums_ref[pl.ds(at, SHARE), :]
            exponents_a.append(encode(block[:, :SPLIT], to_a, k))
            exponents_b.append(encode(block[:, SPLIT:], to_b, k))
    for _, to_a, to_b, exponents_a, exponents_b in targets:
        encode_exponents(exponents_a, to_a)
        encode_exponents(exponents_b, to_b)
    for store in stores:
        store.wait()


def middle_a_kernel(kept, came, own_ref, *sent):
    for i in range(X):
        sums = [decode(kept.at[i], k) + decode(came.at[i], k) for k in range(3)]
        if i == 0:
            for k in range(3):
                own_ref[k] = sums[k]
        else:
            encode_exponents([encode(sums[k], sent[i - 1], k) for k in range(3)], sent[i - 1])


def middle_b_kernel(kept, *refs):
    came, own_ref, sent = refs[:3], refs[3], refs[4]
    for r in range(YL):
        sums = [decode(kept.at[r], k) for k in range(3)]
        for each in came:
            sums = [sums[k] + decode(each.at[r], k) for k in range(3)]
        if r == 0:
            for k in range(3):
                own_ref[k] = sums[k]
        else:
            encode_exponents([encode(sums[k], sent, k) for k in range(3)], sent)


def terms_kernel(own_a, first, second, third, own_b, other, weight_ref, weighted_ref, gate_ref, up_ref):
    totals = []
    for k in range(3):
        total_a = own_a[k] + decode(first, k) + decode(second, k) + decode(third, k)
        totals.append(jnp.concatenate([total_a, own_b[k] + decode(other, k)], axis=1))
    gate, up, back = totals
    weight = weight_ref[...]
    sigmoid_gate = 1.0 / (1.0 + jnp.exp(-gate))
    lifted = gate * sigmoid_gate
    grad_act = weight * back
    weighted_ref[...] = (weight * lifted * up).astype(BF16)
    gate_ref[...] = (grad_act * up * sigmoid_gate * (1.0 + gate * (1.0 - sigmoid_gate))).astype(BF16)
    up_ref[...] = (grad_act * lifted).astype(BF16)


def input_kernel(place_ref, pos_ref, *refs):
    blocks, refs = refs[:12], refs[12:]
    gate_e, gate_d, up_e, up_d, kept_ref, sent_ref, gate_ref, up_ref, total_ref = refs
    c = place_ref[2]
    place_terms(place_ref, blocks[:8], "x", gate_ref)
    place_terms(place_ref, blocks[8:], "yl", up_ref)
    gate, up = gate_ref[...], up_ref[...]
    routed = dot(gate[0:HE, 0:CAP], gate_e[...], (0, 0)) + dot(up[0:HE, 0:CAP], up_e[...], (0, 0))
    high = routed.astype(BF16)
    low = (routed - high.astype(F32)).astype(BF16)
    slots = lax.broadcasted_iota(jnp.int32, (TOKENS, CAP), 1)
    one_hot = jnp.where(slots == pos_ref[...], 1.0, 0.0).astype(BF16)
    total_ref[...] = dot(one_hot, high, (1, 0)) + dot(one_hot, low, (1, 0))
    for q in range(TOKENS // QUARTER):
        rows = slice(q * STRIDE, q * STRIDE + HD)
        dense = dot(gate[rows, CAP:], gate_d[...], (0, 0)) + dot(up[rows, CAP:], up_d[...], (0, 0))
        total_ref[q * QUARTER : (q + 1) * QUARTER, :] += dense
    for i in range(Z * YH):
        mine = pl.multiple_of(i * C * OWN + c * OWN, OWN)
        other = pl.multiple_of(i * C * OWN + (1 - c) * OWN, OWN)
        kept_ref[i] = total_ref[pl.ds(mine, OWN), :]
        sent_ref[i] = total_ref[pl.ds(other, OWN), :].astype(BF16)


def fold_c_kernel(place_ref, kept, came, kept_ref, sent_ref):
    yh = place_ref[1]
    for i in range(Z):
        kept_ref[i] = kept[YH * i + yh] + came[YH * i + yh].astype(F32)
        sent_ref[i] = (kept[YH * i + 1 - yh] + came[YH * i + 1 - yh].astype(F32)).astype(BF16)


def fold_yh_kernel(place_ref, kept, came, own_ref, *sent):
    z = place_ref[0]
    own_ref[...] = kept[z] + came[z].astype(F32)
    for k, to in zip(TO_Z, sent):
        i = lax.rem(z + k, Z)
        to[...] = (kept[i] + came[i].astype(F32)).astype(BF16)


def gate_up_kernel(gate_ref, up_ref, far_tok, far_in, *refs):
    outs, tok_ref, in_ref, tiles, in_sems, out_sems = refs[:4], refs[4], refs[5], refs[6:10], refs[10], refs[11]
    fetches = [pltpu.make_async_copy(far_tok, tok_ref, in_sems.at[0]), pltpu.make_async_copy(far_in, in_ref, in_sems.at[1])]
    products([(gate_ref, in_ref, tok_ref), (up_ref, in_ref, tok_ref)], fetches, outs, tiles, out_sems)


def down_kernel(place_ref, *refs):
    blocks, far_cot, far_back, outs = refs[:4], refs[4], refs[5], refs[6:8]
    down_ref, cot_ref, back_ref, tiles, in_sems, out_sems = refs[8], refs[9], refs[10], refs[11:13], refs[13], refs[14]
    fetches = [pltpu.make_async_copy(far_cot, cot_ref, in_sems.at[0]), pltpu.make_async_copy(far_back, back_ref, in_sems.at[1])]
    place_terms(place_ref, blocks, "yl", down_ref)
    products([(down_ref, back_ref, cot_ref)], fetches, outs, tiles, out_sems)


def products(work, fetches, outs, tiles, sems):
    for fetch in fetches:
        fetch.start()
    for fetch in fetches:
        fetch.wait()
    stores = [pltpu.make_async_copy(tile, out, sems.at[i]) for i, (tile, out) in enumerate(zip(tiles, outs))]
    for i, (value_ref, rows, whole) in enumerate(work):
        tiles[2 * i][...] = dot(value_ref[0:HE, 0:CAP], rows[...], (1, 0))
        stores[2 * i].start()
        dense = jnp.concatenate([value_ref[q * STRIDE : q * STRIDE + HD, CAP:] for q in range(TOKENS // QUARTER)], axis=1)
        tiles[2 * i + 1][...] = dot(dense, whole[...], (1, 0))
        stores[2 * i + 1].start()
    for store in stores:
        store.wait()


def shards(tokens, cotangent, route_ids, route_probs, dense_gate, dense_up, dense_down, expert_gate, expert_up, expert_down):
    expert_number = lax.axis_index(DP) * HE // FF
    place = jnp.stack([lax.axis_index(a) for a in AXES]).astype(jnp.int32)
    smem = pl.BlockSpec(memory_space=pltpu.SMEM)

    chosen = route_ids == expert_number
    member = jnp.any(chosen, axis=1)
    token_weight = jnp.sum(jnp.where(chosen, route_probs, 0.0), axis=1)
    position = jnp.where(member, jnp.cumsum(member.astype(jnp.int32)) - 1, -1)
    slots = lax.broadcasted_iota(jnp.int32, (CAP, TOKENS), 0)
    slot_weight = jnp.sum(jnp.where(slots == position[None, :], token_weight[None, :], 0.0), axis=1)
    weight = jnp.concatenate([slot_weight, jnp.ones((QUARTER,), F32)])[None, :]

    mine, mine_far, across, down, weight = gather_column(jnp.stack([tokens, cotangent]), position[None, :], position[:, None], weight)
    columns = (mine, mine_far, shift(mine, "c", C, 1), shift(mine_far, "c", C, 1))
    gate_e, gate_d, up_e, up_d = expert_gate.T, dense_gate.T, expert_up.T, dense_up.T

    far, vmem = pl.BlockSpec(memory_space=pltpu.HBM), pl.BlockSpec(memory_space=pltpu.VMEM)
    large_params, params = (pltpu.CompilerParams(vmem_limit_bytes=n * MIB) for n in (24, 20))
    sems = pltpu.SemaphoreType.DMA
    small, large = (HD, WIDTH), (HE, WIDTH)
    whole, picked, share = (TOKENS, WIDTH), (CAP, WIDTH), (SHARE, WIDTH)
    left, right = (CODED, SPLIT), (CODED, WIDTH - SPLIT)
    code = jnp.int16
    held = [(large, BF16), (small, BF16)] * 3 + [(whole, BF16)] * 2 + [(picked, BF16)] * 2
    all_tokens, all_grads, rows_in, rows_back, kept_a, sent_a, kept_b, *sent_b = pl.pallas_call(
        forward_kernel,
        out_shape=[shape(*h) for h in held[6:]] + [shape((X, *left), code)] * 2 + [shape((YL, *right), code)] * X,
        in_specs=[smem] + [vmem] * 5 + [far] * 6,
        out_specs=[far] * 4 + [vmem] * 6,
        scratch_shapes=[pltpu.VMEM(*h) for h in held] + [pltpu.VMEM((PARTS * SHARE, WIDTH), F32), sems((6,)), sems((4,))],
        compiler_params=large_params,
        name="forward",
    )(place, across, *columns, gate_e, gate_d, up_e, up_d, expert_down, dense_down)
    came_a = shift(sent_a, "yl", YL, 1)
    came_b = [shift(value, "x", X, away) for value, away in zip(sent_b, TO_X[1:])]
    own_a, *sums_a = pl.pallas_call(
        middle_a_kernel,
        out_shape=[shape((3, SHARE, SPLIT), F32)] + [shape(left, code)] * 3,
        compiler_params=params,
        name="middle_a",
    )(kept_a, came_a)
    *came_b, own_a = lax.optimization_barrier((*came_b, own_a))
    parts_a = [shift(value, "x", X, away) for value, away in zip(sums_a, TO_X[1:])]
    own_b, sum_b = pl.pallas_call(
        middle_b_kernel,
        out_shape=[shape((3, SHARE, WIDTH - SPLIT), F32), shape(right, code)],
        compiler_params=params,
        name="middle_b",
    )(kept_b, *came_b)
    part_b = shift(sum_b, "yl", YL, 1)
    weighted, grad_gate, grad_up = pl.pallas_call(
        terms_kernel,
        out_shape=[shape(share, BF16)] * 3,
        compiler_params=params,
        name="terms",
    )(own_a, *parts_a, own_b, part_b, weight)

    part = (Z * YH, OWN, WIDTH)
    summed = (PARTS * SHARE, WIDTH)
    weighted_pair = jnp.stack([weighted, shift(weighted, "yl", YL, 1)])
    kept, sent, gate_terms, up_terms = pl.pallas_call(
        input_kernel,
        out_shape=[shape(part, F32), shape(part, BF16), shape(summed, BF16), shape(summed, BF16)],
        in_specs=[smem] + [vmem] * 17,
        scratch_shapes=[pltpu.VMEM(whole, F32)],
        compiler_params=params,
        name="input",
    )(place, down, *gather_terms(grad_gate, "x"), *gather_terms(grad_up, "yl"), gate_e, gate_d, up_e, up_d)
    sent, weighted_pair = lax.optimization_barrier((sent, weighted_pair))
    column, block = (Z, OWN, WIDTH), (OWN, WIDTH)
    kept, sent = pl.pallas_call(
        fold_c_kernel,
        out_shape=[shape(column, F32), shape(column, BF16)],
        in_specs=[smem] + [vmem] * 2,
        compiler_params=params,
        name="fold_c",
    )(place, kept, shift(sent, "c", C, 1))
    weighted_terms = gather_pairs(weighted_pair)
    came = shift(sent, "yh", YH, 1)
    pair = [(large, F32), (small, F32)]
    gate_large, gate_small, up_large, up_small = pl.pallas_call(
        gate_up_kernel,
        out_shape=[shape(*h) for h in pair * 2],
        in_specs=[vmem] * 2 + [far] * 2,
        out_specs=[far] * 4,
        scratch_shapes=[pltpu.VMEM(whole, BF16), pltpu.VMEM(picked, BF16)] + [pltpu.VMEM(*h) for h in pair * 2] + [sems((2,)), sems((4,))],
        compiler_params=params,
        name="gate_up",
    )(gate_terms, up_terms, all_tokens, rows_in)
    came, gate_small = lax.optimization_barrier((came, gate_small))
    own, *sent = pl.pallas_call(
        fold_yh_kernel,
        out_shape=[shape(block, F32)] + [shape(block, BF16)] * len(TO_Z),
        in_specs=[smem] + [vmem] * 2,
        compiler_params=params,
        name="fold_yh",
    )(place, kept, came)
    came = [shift(value, "z", Z, k) for value, k in zip(sent, TO_Z)]
    input_grad = own
    for value in came:
        input_grad = input_grad + value.astype(F32)

    down_large, down_small = pl.pallas_call(
        down_kernel,
        out_shape=[shape(*h) for h in pair],
        in_specs=[smem] + [vmem] * 4 + [far] * 2,
        out_specs=[far] * 2,
        scratch_shapes=[pltpu.VMEM(summed, BF16), pltpu.VMEM(whole, BF16), pltpu.VMEM(picked, BF16)]
        + [pltpu.VMEM(*h) for h in pair]
        + [sems((2,)), sems((2,))],
        compiler_params=params,
        name="down",
    )(place, *weighted_terms, all_grads, rows_back)
    return (input_grad, gate_small.T, up_small.T, down_small, gate_large.T, up_large.T, down_large)


def solution(mesh):
    fine = Mesh(mesh.devices.reshape(SIZES), AXES)
    rows, cols = P(DP, EX), P(EX, DP)
    in_specs = (rows, rows, P(), P(), cols, cols, rows, cols, cols, rows)
    out_specs = (rows, cols, cols, rows, cols, cols, rows)
    return jax.shard_map(shards, mesh=fine, in_specs=in_specs, out_specs=out_specs, check_vma=False)
```

```python
import jax
import jax.numpy as jnp
from jax import lax
from jax.experimental import pallas as pl
from jax.experimental.pallas import tpu as pltpu
from jax.sharding import Mesh, PartitionSpec as P

FF = 4864
Z, YH, C, YL, X = 8, 2, 2, 2, 4
AXES = ("z", "yh", "c", "yl", "x")
SIZES = (Z, YH, C, YL, X)
DP = ("z", "yh", "c")
EX = ("yl", "x")
PARTS = YL * X
F32 = jnp.float32
BF16 = jnp.bfloat16
TOKENS, CAP, WIDTH = 1024, 640, 896
HE, HD = 608, 152
QUARTER = 256
STRIDE = 160
SHARE = 80
BLOCK = 3 * SHARE
CODED = BLOCK + 16
OWN = 32
SPLIT = 512
MIB = 1024 * 1024


def dot(left, right, dims):
    return lax.dot_general(left, right, ((dims[:1], dims[1:]), ((), ())), preferred_element_type=F32)


def shape(dims, kind):
    return jax.ShapeDtypeStruct(dims, kind)


def shift(value, axis, size, step):
    return lax.ppermute(value, axis, [(i, (i + step) % size) for i in range(size)])


def gather_column(own, *others):
    pair = jnp.stack([own, shift(own, "yh", YH, 1)])
    pieces = [pair]
    below, above = pair, pair
    for step in range(Z // 2 - 1):
        below, above = shift(below, "z", Z, 1), shift(above, "z", Z, -1)
        if step == 1:
            below, above, *others = lax.optimization_barrier((below, above, *others))
        pieces += [below, above]
    return jnp.concatenate([*pieces, shift(below[:1], "z", Z, 1), shift(above[1:], "z", Z, -1)]), *others


def gather_terms(value, first):
    if first == "x":
        near = [value, shift(value, "x", X, 1), shift(value, "x", X, -1), shift(value, "x", X, 2)]
        return [v[None] for v in near + [shift(v, "yl", YL, 1) for v in near]]
    return gather_pairs(jnp.stack([value, shift(value, "yl", YL, 1)]))


def gather_pairs(pair):
    return [pair, shift(pair, "x", X, 1), shift(pair, "x", X, -1), shift(pair, "x", X, 2)]


FROM_X = (0, -1, 1, 2)
TO_X = (0, 1, -1, 2)
TO_Z = (4, 3, 5, 2, 6, 1, 7)
RELATIVE = {
    "x": [[(r, k)] for r in range(YL) for k in FROM_X],
    "yl": [[(0, k), (1, k)] for k in FROM_X],
}
FROM_Z = (0, -1, 1, -2, 2, -3, 3, 4)


def place_terms(place_ref, blocks, first, to_ref):
    yl, x = place_ref[3], place_ref[4]
    for block, origins in zip(blocks, RELATIVE[first]):
        for i, (row, away) in enumerate(origins):
            j = lax.rem(yl + row, YL) * X + lax.rem(x + away + X, X)
            to_ref[pl.ds(pl.multiple_of(j * SHARE, SHARE), SHARE), :] = block[i]


def encode(value, to, k):
    largest = jnp.maximum(jnp.max(jnp.abs(value), axis=0, keepdims=True), 1e-30)
    exponent = jnp.ceil(jnp.log2(largest) + 1e-3)
    coded = jnp.round(value * jnp.exp2(15.0 - exponent))
    to[k * SHARE : (k + 1) * SHARE, :] = coded.astype(jnp.int32).astype(jnp.int16)
    return exponent


def encode_exponents(exponents, to):
    row = lax.broadcasted_iota(jnp.int32, (CODED - BLOCK, exponents[0].shape[1]), 0)
    tile = jnp.where(row == 0, exponents[0], jnp.where(row == 1, exponents[1], exponents[2]))
    to[BLOCK:, :] = tile.astype(jnp.int32).astype(jnp.int16)


def decode(coded, k):
    exponent = coded[BLOCK:, :].astype(jnp.int32).astype(F32)[k : k + 1]
    return coded[k * SHARE : (k + 1) * SHARE, :].astype(jnp.int32).astype(F32) * jnp.exp2(exponent - 15.0)


def forward_kernel(place_ref, pos_ref, mine_ref, sibling_ref, *refs):
    far_weights, far_rows = refs[:6], refs[6:10]
    kept_a, sent_a, sent_b = refs[10], refs[11], refs[12:16]
    weights, rows, sums_ref, in_sems, out_sems = refs[16:22], refs[22:26], refs[26], refs[27], refs[28]
    tok_ref, cot_ref, in_ref, back_ref = rows
    weights_e, weights_d = weights[0:6:2], weights[1:6:2]
    fetches = [pltpu.make_async_copy(far, near, in_sems.at[i]) for i, (far, near) in enumerate(zip(far_weights, weights))]
    stores = [pltpu.make_async_copy(near, far, out_sems.at[i]) for i, (near, far) in enumerate(zip(rows, far_rows))]
    for fetch in fetches:
        fetch.start()
    z, yh, c = place_ref[0], place_ref[1], place_ref[2]
    yl, x = place_ref[3], place_ref[4]
    for core, column in enumerate((mine_ref, sibling_ref)):
        for k, away in enumerate(FROM_Z):
            for r in range(YH):
                at = lax.rem(z + away + Z, Z) * (YH * C * OWN) + lax.rem(yh + r, YH) * (C * OWN) + lax.rem(c + core, C) * OWN
                at = pl.multiple_of(at, OWN)
                tok_ref[pl.ds(at, OWN), :] = column[YH * k + r, 0]
                cot_ref[pl.ds(at, OWN), :] = column[YH * k + r, 1]
    slots = lax.broadcasted_iota(jnp.int32, (CAP, TOKENS), 0)
    one_hot = jnp.where(slots == pos_ref[...], 1.0, 0.0).astype(BF16)
    for first in range(0, CAP, QUARTER):
        last = min(first + QUARTER, CAP)
        some = one_hot[first:last, first:]
        in_ref[first:last, :] = dot(some, tok_ref[first:, :], (1, 0)).astype(BF16)
        back_ref[first:last, :] = dot(some, cot_ref[first:, :], (1, 0)).astype(BF16)
    for store in stores:
        store.start()
    targets = []
    for r in range(YL):
        for i, away in enumerate(TO_X):
            j = lax.rem(yl + r, YL) * X + lax.rem(x + away + X, X)
            to_a, to_b = (sent_a if r else kept_a).at[i], sent_b[i].at[r]
            targets.append((pl.multiple_of(j * SHARE, SHARE), to_a, to_b, [], []))
    for k in range(3):
        picked, whole = (back_ref, cot_ref) if k == 2 else (in_ref, tok_ref)
        fetches[2 * k].wait()
        fetches[2 * k + 1].wait()
        sums_ref[0:HE, 0:CAP] = dot(weights_e[k][...], picked[...], (1, 1))
        sums_ref[HE:, 0:CAP] = jnp.zeros((PARTS * SHARE - HE, CAP), F32)
        dense = dot(weights_d[k][...], whole[...], (1, 1))
        for q in range(TOKENS // QUARTER):
            sums_ref[q * STRIDE : q * STRIDE + HD, CAP:] = dense[:, q * QUARTER : (q + 1) * QUARTER]
            sums_ref[q * STRIDE + HD : (q + 1) * STRIDE, CAP:] = jnp.zeros((STRIDE - HD, QUARTER), F32)
        for at, to_a, to_b, exponents_a, exponents_b in targets:
            block = sums_ref[pl.ds(at, SHARE), :]
            exponents_a.append(encode(block[:, :SPLIT], to_a, k))
            exponents_b.append(encode(block[:, SPLIT:], to_b, k))
    for _, to_a, to_b, exponents_a, exponents_b in targets:
        encode_exponents(exponents_a, to_a)
        encode_exponents(exponents_b, to_b)
    for store in stores:
        store.wait()


def middle_a_kernel(kept, came, own_ref, *sent):
    for i in range(X):
        sums = [decode(kept.at[i], k) + decode(came.at[i], k) for k in range(3)]
        if i == 0:
            for k in range(3):
                own_ref[k] = sums[k]
        else:
            encode_exponents([encode(sums[k], sent[i - 1], k) for k in range(3)], sent[i - 1])


def middle_b_kernel(kept, *refs):
    came, own_ref, sent = refs[:3], refs[3], refs[4]
    for r in range(YL):
        sums = [decode(kept.at[r], k) for k in range(3)]
        for each in came:
            sums = [sums[k] + decode(each.at[r], k) for k in range(3)]
        if r == 0:
            for k in range(3):
                own_ref[k] = sums[k]
        else:
            encode_exponents([encode(sums[k], sent, k) for k in range(3)], sent)


def terms_kernel(own_a, first, second, third, own_b, other, weight_ref, weighted_ref, gate_ref, up_ref):
    totals = []
    for k in range(3):
        total_a = own_a[k] + decode(first, k) + decode(second, k) + decode(third, k)
        totals.append(jnp.concatenate([total_a, own_b[k] + decode(other, k)], axis=1))
    gate, up, back = totals
    weight = weight_ref[...]
    sigmoid_gate = 1.0 / (1.0 + jnp.exp(-gate))
    lifted = gate * sigmoid_gate
    grad_act = weight * back
    weighted_ref[...] = (weight * lifted * up).astype(BF16)
    gate_ref[...] = (grad_act * up * sigmoid_gate * (1.0 + gate * (1.0 - sigmoid_gate))).astype(BF16)
    up_ref[...] = (grad_act * lifted).astype(BF16)


def input_kernel(place_ref, pos_ref, *refs):
    blocks, refs = refs[:12], refs[12:]
    gate_e, gate_d, up_e, up_d, kept_ref, sent_ref, gate_ref, up_ref, total_ref = refs
    c = place_ref[2]
    place_terms(place_ref, blocks[:8], "x", gate_ref)
    place_terms(place_ref, blocks[8:], "yl", up_ref)
    gate, up = gate_ref[...], up_ref[...]
    routed = dot(gate[0:HE, 0:CAP], gate_e[...], (0, 0)) + dot(up[0:HE, 0:CAP], up_e[...], (0, 0))
    high = routed.astype(BF16)
    low = (routed - high.astype(F32)).astype(BF16)
    slots = lax.broadcasted_iota(jnp.int32, (TOKENS, CAP), 1)
    one_hot = jnp.where(slots == pos_ref[...], 1.0, 0.0).astype(BF16)
    for q in range(TOKENS // QUARTER):
        rows = slice(q * STRIDE, q * STRIDE + HD)
        dense = dot(gate[rows, CAP:], gate_d[...], (0, 0)) + dot(up[rows, CAP:], up_d[...], (0, 0))
        last = min((q + 1) * QUARTER, CAP)
        some = one_hot[q * QUARTER : (q + 1) * QUARTER, :last]
        total_ref[q * QUARTER : (q + 1) * QUARTER, :] = dense + dot(some, high[:last], (1, 0)) + dot(some, low[:last], (1, 0))
    for i in range(Z * YH):
        mine = pl.multiple_of(i * C * OWN + c * OWN, OWN)
        other = pl.multiple_of(i * C * OWN + (1 - c) * OWN, OWN)
        kept_ref[i] = total_ref[pl.ds(mine, OWN), :]
        sent_ref[i] = total_ref[pl.ds(other, OWN), :].astype(BF16)


def fold_c_kernel(place_ref, kept, came, kept_ref, sent_ref):
    yh = place_ref[1]
    for i in range(Z):
        kept_ref[i] = kept[YH * i + yh] + came[YH * i + yh].astype(F32)
        sent_ref[i] = (kept[YH * i + 1 - yh] + came[YH * i + 1 - yh].astype(F32)).astype(BF16)


def fold_yh_kernel(place_ref, kept, came, own_ref, *sent):
    z = place_ref[0]
    own_ref[...] = kept[z] + came[z].astype(F32)
    for k, to in zip(TO_Z, sent):
        i = lax.rem(z + k, Z)
        to[...] = (kept[i] + came[i].astype(F32)).astype(BF16)


def gate_up_kernel(gate_ref, up_ref, far_tok, far_in, *refs):
    outs, tok_ref, in_ref, tiles, in_sems, out_sems = refs[:4], refs[4], refs[5], refs[6:10], refs[10], refs[11]
    fetches = [pltpu.make_async_copy(far_tok, tok_ref, in_sems.at[0]), pltpu.make_async_copy(far_in, in_ref, in_sems.at[1])]
    products([(gate_ref, in_ref, tok_ref), (up_ref, in_ref, tok_ref)], fetches, outs, tiles, out_sems)


def down_kernel(place_ref, *refs):
    blocks, far_cot, far_back, outs = refs[:4], refs[4], refs[5], refs[6:8]
    down_ref, cot_ref, back_ref, tiles, in_sems, out_sems = refs[8], refs[9], refs[10], refs[11:13], refs[13], refs[14]
    fetches = [pltpu.make_async_copy(far_cot, cot_ref, in_sems.at[0]), pltpu.make_async_copy(far_back, back_ref, in_sems.at[1])]
    place_terms(place_ref, blocks, "yl", down_ref)
    products([(down_ref, back_ref, cot_ref)], fetches, outs, tiles, out_sems)


def products(work, fetches, outs, tiles, sems):
    for fetch in fetches:
        fetch.start()
    for fetch in fetches:
        fetch.wait()
    stores = [pltpu.make_async_copy(tile, out, sems.at[i]) for i, (tile, out) in enumerate(zip(tiles, outs))]
    for i, (value_ref, rows, whole) in enumerate(work):
        tiles[2 * i][...] = dot(value_ref[0:HE, 0:CAP], rows[...], (1, 0))
        stores[2 * i].start()
        dense = jnp.concatenate([value_ref[q * STRIDE : q * STRIDE + HD, CAP:] for q in range(TOKENS // QUARTER)], axis=1)
        tiles[2 * i + 1][...] = dot(dense, whole[...], (1, 0))
        stores[2 * i + 1].start()
    for store in stores:
        store.wait()


def shards(tokens, cotangent, route_ids, route_probs, dense_gate, dense_up, dense_down, expert_gate, expert_up, expert_down):
    expert_number = lax.axis_index(DP) * HE // FF
    place = jnp.stack([lax.axis_index(a) for a in AXES]).astype(jnp.int32)
    smem = pl.BlockSpec(memory_space=pltpu.SMEM)

    chosen = route_ids == expert_number
    member = jnp.any(chosen, axis=1)
    token_weight = jnp.sum(jnp.where(chosen, route_probs, 0.0), axis=1)
    position = jnp.where(member, jnp.cumsum(member.astype(jnp.int32)) - 1, -1)
    slots = lax.broadcasted_iota(jnp.int32, (CAP, TOKENS), 0)
    slot_weight = jnp.sum(jnp.where(slots == position[None, :], token_weight[None, :], 0.0), axis=1)
    weight = jnp.concatenate([slot_weight, jnp.ones((QUARTER,), F32)])[None, :]

    mine, across, down, weight = gather_column(jnp.stack([tokens, cotangent]), position[None, :], position[:, None], weight)
    columns = (mine, shift(mine, "c", C, 1))
    gate_e, gate_d, up_e, up_d = expert_gate.T, dense_gate.T, expert_up.T, dense_up.T

    far, vmem = pl.BlockSpec(memory_space=pltpu.HBM), pl.BlockSpec(memory_space=pltpu.VMEM)
    large_params, params = (pltpu.CompilerParams(vmem_limit_bytes=n * MIB) for n in (24, 20))
    sems = pltpu.SemaphoreType.DMA
    small, large = (HD, WIDTH), (HE, WIDTH)
    whole, picked, share = (TOKENS, WIDTH), (CAP, WIDTH), (SHARE, WIDTH)
    left, right = (CODED, SPLIT), (CODED, WIDTH - SPLIT)
    code = jnp.int16
    held = [(large, BF16), (small, BF16)] * 3 + [(whole, BF16)] * 2 + [(picked, BF16)] * 2
    all_tokens, all_grads, rows_in, rows_back, kept_a, sent_a, kept_b, *sent_b = pl.pallas_call(
        forward_kernel,
        out_shape=[shape(*h) for h in held[6:]] + [shape((X, *left), code)] * 2 + [shape((YL, *right), code)] * X,
        in_specs=[smem] + [vmem] * 3 + [far] * 6,
        out_specs=[far] * 4 + [vmem] * 6,
        scratch_shapes=[pltpu.VMEM(*h) for h in held] + [pltpu.VMEM((PARTS * SHARE, WIDTH), F32), sems((6,)), sems((4,))],
        compiler_params=large_params,
        name="forward",
    )(place, across, *columns, gate_e, gate_d, up_e, up_d, expert_down, dense_down)
    came_a = shift(sent_a, "yl", YL, 1)
    came_b = [shift(value, "x", X, away) for value, away in zip(sent_b, TO_X[1:])]
    own_a, *sums_a = pl.pallas_call(
        middle_a_kernel,
        out_shape=[shape((3, SHARE, SPLIT), F32)] + [shape(left, code)] * 3,
        compiler_params=params,
        name="middle_a",
    )(kept_a, came_a)
    *came_b, own_a = lax.optimization_barrier((*came_b, own_a))
    parts_a = [shift(value, "x", X, away) for value, away in zip(sums_a, TO_X[1:])]
    own_b, sum_b = pl.pallas_call(
        middle_b_kernel,
        out_shape=[shape((3, SHARE, WIDTH - SPLIT), F32), shape(right, code)],
        compiler_params=params,
        name="middle_b",
    )(kept_b, *came_b)
    part_b = shift(sum_b, "yl", YL, 1)
    weighted, grad_gate, grad_up = pl.pallas_call(
        terms_kernel,
        out_shape=[shape(share, BF16)] * 3,
        compiler_params=params,
        name="terms",
    )(own_a, *parts_a, own_b, part_b, weight)

    part = (Z * YH, OWN, WIDTH)
    summed = (PARTS * SHARE, WIDTH)
    weighted_pair = jnp.stack([weighted, shift(weighted, "yl", YL, 1)])
    kept, sent, gate_terms, up_terms = pl.pallas_call(
        input_kernel,
        out_shape=[shape(part, F32), shape(part, BF16), shape(summed, BF16), shape(summed, BF16)],
        in_specs=[smem] + [vmem] * 17,
        scratch_shapes=[pltpu.VMEM(whole, F32)],
        compiler_params=params,
        name="input",
    )(place, down, *gather_terms(grad_gate, "x"), *gather_terms(grad_up, "yl"), gate_e, gate_d, up_e, up_d)
    sent, weighted_pair = lax.optimization_barrier((sent, weighted_pair))
    column, block = (Z, OWN, WIDTH), (OWN, WIDTH)
    kept, sent = pl.pallas_call(
        fold_c_kernel,
        out_shape=[shape(column, F32), shape(column, BF16)],
        in_specs=[smem] + [vmem] * 2,
        compiler_params=params,
        name="fold_c",
    )(place, kept, shift(sent, "c", C, 1))
    weighted_terms = gather_pairs(weighted_pair)
    came = shift(sent, "yh", YH, 1)
    pair = [(large, F32), (small, F32)]
    gate_large, gate_small, up_large, up_small = pl.pallas_call(
        gate_up_kernel,
        out_shape=[shape(*h) for h in pair * 2],
        in_specs=[vmem] * 2 + [far] * 2,
        out_specs=[far] * 4,
        scratch_shapes=[pltpu.VMEM(whole, BF16), pltpu.VMEM(picked, BF16)] + [pltpu.VMEM(*h) for h in pair * 2] + [sems((2,)), sems((4,))],
        compiler_params=params,
        name="gate_up",
    )(gate_terms, up_terms, all_tokens, rows_in)
    came, gate_small = lax.optimization_barrier((came, gate_small))
    own, *sent = pl.pallas_call(
        fold_yh_kernel,
        out_shape=[shape(block, F32)] + [shape(block, BF16)] * len(TO_Z),
        in_specs=[smem] + [vmem] * 2,
        compiler_params=params,
        name="fold_yh",
    )(place, kept, came)
    came = [shift(value, "z", Z, k) for value, k in zip(sent, TO_Z)]
    input_grad = own
    for value in came:
        input_grad = input_grad + value.astype(F32)

    down_large, down_small = pl.pallas_call(
        down_kernel,
        out_shape=[shape(*h) for h in pair],
        in_specs=[smem] + [vmem] * 4 + [far] * 2,
        out_specs=[far] * 2,
        scratch_shapes=[pltpu.VMEM(summed, BF16), pltpu.VMEM(whole, BF16), pltpu.VMEM(picked, BF16)]
        + [pltpu.VMEM(*h) for h in pair]
        + [sems((2,)), sems((2,))],
        compiler_params=params,
        name="down",
    )(place, *weighted_terms, all_grads, rows_back)
    return (input_grad, gate_small.T, up_small.T, down_small, gate_large.T, up_large.T, down_large)


def solution(mesh):
    fine = Mesh(mesh.devices.reshape(SIZES), AXES)
    rows, cols = P(DP, EX), P(EX, DP)
    in_specs = (rows, rows, P(), P(), cols, cols, rows, cols, cols, rows)
    out_specs = (rows, cols, cols, rows, cols, cols, rows)
    return jax.shard_map(shards, mesh=fine, in_specs=in_specs, out_specs=out_specs, check_vma=False)
```
